32 devices in a mesh: wide: 8 (over z, x), tensor: 4 (over y, core).
Axes of the slice: x: 2, y: 2, z: 4, core: 2. Of those that a mesh axis runs over, the one named last changes fastest.
Arguments:
- tokens: bfloat16 [4096, 8192], P('wide', 'tensor'), may hold values from -6 to 6
- key_value_weight: bfloat16 [8192, 2048], P(None, 'tensor'), may hold values from -0.0625 to 0.0625
- adapter_down_maps: bfloat16 [8192, 128, 64], P('tensor', 'wide'), may hold values from -0.0625 to 0.0625
- adapter_up_maps: bfloat16 [128, 64, 2048], P('wide', None, 'tensor'), may hold values from -0.75 to 0.75
- adapter_per_row: int32 [4096], P('wide'), may hold values from 0 to 127, as said below
- adapter_storage_slot: int32 [128], replicated, may hold values from 0 to 127, as said below
Outputs:
- kv_out: bfloat16 [4096, 2048], P('wide', 'tensor')
The draws below stay inside these ranges and needn't reach their ends.
Inputs may be any that keep to these rules, and one draw needn't show every extreme that they name: `adapter_per_row`: the adapter stored at position p belongs to owner p // 16 of wide. Among the 512 rows of one index of wide, at most 128 name adapters of one owner; in every draw one owner gets exactly 128 rows from every index of wide. `adapter_storage_slot`: each position is taken by exactly one adapter.
All inputs are finite; a program needn't handle non-finite values.
Results may differ from the reference program's by a relative error of at most 0.0049.
Values may be sent and summed in bfloat16 or wider, within the bound.
A program may use at most 64 MiB of HBM per device.

```python
import jax
import jax.numpy as jnp
from jax import lax

MODEL_WIDTH = 8192
KEY_VALUE_COLUMNS = 2048
ADAPTER_RANK = 64
TOK_DEV = 512
ADP_DEV = 16
TOKENS = 4096
ADAPTER_COUNT = 128
CAP = 128


def common_draw(key):
    base_key = jax.random.fold_in(key, 7)
    wide_count = TOKENS // TOK_DEV
    place = jax.random.permutation(jax.random.fold_in(base_key, 1), ADAPTER_COUNT).astype(jnp.int32)
    hottest = jax.random.randint(jax.random.fold_in(base_key, 2), (), 0, wide_count)

    def block_positions(block):
        block_key = jax.random.fold_in(base_key, 100 + block)
        others = jax.random.permutation(jax.random.fold_in(block_key, 1), (wide_count - 1) * CAP)[:TOK_DEV - CAP] + CAP
        virtual = jnp.concatenate([jnp.arange(CAP, dtype=jnp.int32), others.astype(jnp.int32)])
        virtual = jax.random.permutation(jax.random.fold_in(block_key, 2), virtual)
        owner_index = (virtual // CAP + hottest) % wide_count
        local_index = jax.random.randint(jax.random.fold_in(block_key, 3), (TOK_DEV,), 0, ADP_DEV)
        return (owner_index * ADP_DEV + local_index).astype(jnp.int32)
    positions = jax.vmap(block_positions)(jnp.arange(wide_count)).reshape(TOKENS)
    inverse = jnp.zeros((ADAPTER_COUNT,), jnp.int32).at[place].set(jnp.arange(ADAPTER_COUNT, dtype=jnp.int32))
    return (place, inverse[positions].astype(jnp.int32))


def draw_adapter_per_row(key, part):
    return common_draw(key)[1]


def draw_adapter_storage_slot(key, part):
    return common_draw(key)[0]


def shard_levels(stream_key, shape, cuts, least, high):
    def one(axis_at, parts):
        steps = jax.random.uniform(jax.random.fold_in(jax.random.fold_in(stream_key, 6), axis_at), (parts,), jnp.float32, least / len(cuts), high / len(cuts))
        return jnp.repeat(jnp.exp(steps), shape[axis_at] // parts).reshape((-1,) + (1,) * (len(shape) - axis_at - 1))

    gain = one(*cuts[0])
    for cut in cuts[1:]:
        gain = gain * one(*cut)
    return gain


def centred(rng, shape, width, bound, split=(), kind=jnp.bfloat16):
    values = width * jax.random.normal(rng, shape, jnp.float32)
    if split:
        values = values * shard_levels(rng, shape, split, -0.22, 0.18)
    return jnp.clip(values, -bound, bound).astype(kind)


def setup_inputs(seed: int = 0) -> dict:
    key_of = jax.random.split(jax.random.key(seed), 7)
    return {
        "tokens": centred(key_of[0], (TOKENS, MODEL_WIDTH), 1.0, 6.0, ((0, 8), (1, 4))),
        "key_value_weight": centred(key_of[1], (MODEL_WIDTH, KEY_VALUE_COLUMNS), MODEL_WIDTH ** -0.5, 0.0625, ((1, 4),)),
        "adapter_down_maps": centred(key_of[2], (MODEL_WIDTH, ADAPTER_COUNT, ADAPTER_RANK), MODEL_WIDTH ** -0.5, 0.0625, ((0, 4), (1, 8))),
        "adapter_up_maps": centred(key_of[3], (ADAPTER_COUNT, ADAPTER_RANK, KEY_VALUE_COLUMNS), ADAPTER_RANK ** -0.5, 0.75, ((0, 8), (2, 4))),
        "adapter_per_row": draw_adapter_per_row(jax.random.fold_in(key_of[6], 71), 0),
        "adapter_storage_slot": draw_adapter_storage_slot(jax.random.fold_in(key_of[6], 71), 0),
    }


def reference(tokens, key_value_weight, adapter_down_maps, adapter_up_maps, adapter_per_row, adapter_storage_slot):
    base_projection_output = jnp.dot(tokens, key_value_weight, preferred_element_type=jnp.float32)
    storage_position = adapter_storage_slot[adapter_per_row].astype(jnp.int32)

    def single_row(pair):
        token_row, storage_index = pair
        down_matrix = lax.dynamic_index_in_dim(adapter_down_maps, storage_index, 1, keepdims=False)
        reduced_rows = jnp.dot(token_row[None, :], down_matrix, preferred_element_type=jnp.float32).astype(jnp.bfloat16)
        up_matrix = lax.dynamic_index_in_dim(adapter_up_maps, storage_index, 0, keepdims=False)
        adapter_correction = jnp.dot(reduced_rows, up_matrix, preferred_element_type=jnp.float32).astype(jnp.bfloat16)
        return adapter_correction[0]

    adapter_correction = lax.map(single_row, (tokens, storage_position))
    return (base_projection_output + adapter_correction.astype(jnp.float32)).astype(jnp.bfloat16)
```

```python
import functools

import jax
import jax.numpy as jnp
from jax import lax
from jax.experimental import pallas as pl
from jax.experimental.pallas import tpu as pltpu
from jax.sharding import PartitionSpec as P

MESH = pl.DeviceIdType.MESH
F32 = jnp.float32
BF16 = jnp.bfloat16
LANES = 128


def flip(index, mask, count):
    out, bit = 0, 1
    while bit < count:
        out = out + ((index // bit + mask // bit) % 2) * bit
        bit *= 2
    return out


def iota(shape, dim):
    return lax.broadcasted_iota(jnp.int32, shape, dim)


def to_column(row, size):
    eye = iota((size, row.shape[1]), 0) == iota((size, row.shape[1]), 1)
    return jnp.sum(jnp.where(eye, row, 0.0), axis=1, keepdims=True)


def kernel(
    W,
    T,
    cap,
    per_owner,
    rank,
    tok,
    w_hbm,
    dn_hbm,
    up_hbm,
    apr,
    table,
    out,
    w,
    dn,
    up,
    gat,
    acc,
    rows_out,
    rows_in,
    loc_out,
    loc_in,
    part_out,
    part_in,
    delta_out,
    delta_in,
    load_sem,
    gat_s,
    gat_r,
    row_s,
    row_r,
    loc_s,
    loc_r,
    part_s,
    part_r,
    delta_s,
    delta_r,
):
    me = lax.axis_index("wide")
    te = lax.axis_index("tensor")
    R, F = tok.shape
    C = out.shape[1]
    A = table.shape[1]

    def wide_peer(k):
        return (flip(me, k, W), te)

    def tensor_peer(j):
        return (me, flip(te, j, T))

    barrier = pltpu.get_barrier_semaphore()

    def greet_wide(k, c):
        pl.semaphore_signal(barrier, inc=1, device_id=wide_peer(k), device_id_type=MESH)
        return c

    def greet_tensor(j, c):
        pl.semaphore_signal(barrier, inc=1, device_id=tensor_peer(j), device_id_type=MESH)
        return c

    lax.fori_loop(1, W, greet_wide, 0)
    lax.fori_loop(1, T, greet_tensor, 0)

    load_dn = pltpu.make_async_copy(dn_hbm, dn, load_sem.at[0])
    load_w = pltpu.make_async_copy(w_hbm, w, load_sem.at[1])
    load_up = pltpu.make_async_copy(up_hbm, up, load_sem.at[2])
    load_dn.start()
    load_w.start()
    load_up.start()

    entry = to_column(table[...].astype(F32), A)
    position = jnp.sum(jnp.where(iota((A, R), 0) == apr[...], entry, 0.0), axis=0, keepdims=True)
    owners = max(W, 16)
    owner_id = iota((owners, R), 0).astype(F32)
    hot = jnp.where(
        (position >= owner_id * per_owner) & (position < (owner_id + 1.0) * per_owner), 1.0, 0.0
    )
    before = jnp.where(iota((R, R), 0) < iota((R, R), 1), 1.0, 0.0).astype(BF16)
    earlier = jnp.dot(hot.astype(BF16), before, preferred_element_type=F32)
    owner = jnp.sum(hot * owner_id, axis=0, keepdims=True)
    slot = jnp.sum(hot * earlier, axis=0, keepdims=True) + owner * cap
    local = jnp.broadcast_to(position - owner * per_owner, (16, R)).astype(BF16)
    slot_column = to_column(slot, R)

    pl.semaphore_wait(barrier, W + T - 2)

    def gather(j, src, dst, peer):
        return pltpu.make_async_remote_copy(
            src_ref=src,
            dst_ref=gat.at[dst],
            send_sem=gat_s.at[j],
            recv_sem=gat_r.at[dst],
            device_id=tensor_peer(peer),
            device_id_type=MESH,
        )

    for j in range(2, T, 2):
        gather(j, tok, j, j).start()
    gather(1, tok, 1, 1).start()

    def row_copy(k):
        return pltpu.make_async_remote_copy(
            src_ref=rows_out.at[k],
            dst_ref=rows_in.at[k],
            send_sem=row_s.at[k],
            recv_sem=row_r.at[k],
            device_id=wide_peer(k),
            device_id_type=MESH,
        )

    def loc_copy(k):
        return pltpu.make_async_remote_copy(
            src_ref=loc_out.at[k],
            dst_ref=loc_in.at[k],
            send_sem=loc_s.at[k],
            recv_sem=loc_r.at[k],
            device_id=wide_peer(k),
            device_id_type=MESH,
        )

    def part_copy(k, j):
        return pltpu.make_async_remote_copy(
            src_ref=part_out.at[k],
            dst_ref=part_in.at[k, j],
            send_sem=part_s.at[k, j],
            recv_sem=part_r.at[k, j],
            device_id=tensor_peer(j),
            device_id_type=MESH,
        )

    def delta_copy(k):
        return pltpu.make_async_remote_copy(
            src_ref=delta_out.at[k],
            dst_ref=delta_in.at[k],
            send_sem=delta_s.at[k],
            recv_sem=delta_r.at[k],
            device_id=wide_peer(k),
            device_id_type=MESH,
        )

    def build(k, rows, loc):
        d = flip(me, k, W)
        size = max(cap, LANES)
        pick = jnp.where(
            (iota((size, R), 0) + d * cap).astype(F32) == slot, 1.0, 0.0
        ).astype(BF16)
        loc[k] = lax.dot_general(
            local, pick, (((1,), (1,)), ((), ())), preferred_element_type=F32
        )[:8, :LANES]
        step = min(512, F)
        for c in range(0, F, step):
            rows[k, :, c : c + step] = jnp.dot(
                pick[:cap], tok[:, c : c + step], preferred_element_type=F32
            ).astype(BF16)

    def send(k, c):
        build(k, rows_out, loc_out)
        loc_copy(k).start()
        row_copy(k).start()
        return c

    lax.fori_loop(W // 2, W, send, 0)
    lax.fori_loop(1, W // 2, send, 0)
    build(0, rows_in, loc_in)

    tile = min(256, C)

    def base(j, src, first):
        start = pl.multiple_of(flip(te, j, T) * F, F)

        def columns(n, c):
            cols = pl.ds(pl.multiple_of(n * tile, tile), tile)
            value = jnp.dot(src[...], w[pl.ds(start, F), cols], preferred_element_type=F32)
            if first:
                acc[:, cols] = value
            else:
                acc[:, cols] += value
            return c

        lax.fori_loop(0, C // tile, columns, 0)

    half = cap // 2
    lane = iota((cap, LANES), 1)
    upper = (lane >= rank).astype(F32)
    pairs = per_owner * rank // LANES

    def place(k):
        column = to_column(loc_in[k][:1, :], cap)
        pair = jnp.floor(column * 0.5)
        own = jnp.broadcast_to(column - 2.0 * pair, (cap, LANES)) == upper
        return pair, own

    def shrink(k, c):
        pair, own = place(k)
        total = jnp.zeros((cap, LANES), F32)
        for a in range(0, pairs, 2):
            value = jnp.dot(
                rows_in[k], dn[:, a * LANES : (a + 2) * LANES], preferred_element_type=F32
            )
            total += jnp.where(pair == a, value[:, :LANES], 0.0)
            total += jnp.where(pair == a + 1, value[:, LANES:], 0.0)
        total = jnp.where(own, total, 0.0)
        total += pltpu.roll(total, rank, 1)
        part_out[k] = jnp.where(lane[:half] < rank, total[:half], total[half:])

        def start(j, c):
            part_copy(k, j).start()
            return c

        return lax.fori_loop(1, T, start, c)

    def expand(k):
        def add(j, total):
            part_copy(k, j).wait_recv()
            return total + part_in[k, j]

        total = lax.fori_loop(1, T, add, part_out[k])
        other = pltpu.roll(total, rank, 1)
        low = lane[:half] < rank
        both = jnp.concatenate(
            [jnp.where(low, total, other), jnp.where(low, other, total)], axis=0
        )
        pair, own = place(k)
        both = jnp.where(own, both, 0.0)
        wide = jnp.concatenate(
            [jnp.where(pair == a, both, 0.0).astype(BF16) for a in range(pairs)], axis=1
        )
        return jnp.dot(wide, up[...], preferred_element_type=F32).astype(BF16)

    def arrive(k, c):
        loc_copy(k).wait_recv()
        row_copy(k).wait_recv()
        return shrink(k, c)

    def reply(k, c):
        delta_out[k] = expand(k)
        delta_copy(k).start()
        return c

    def add_delta(k, c):
        d = flip(me, k, W)
        pick = jnp.where(
            (iota((R, cap), 1) + d * cap).astype(F32) == slot_column, 1.0, 0.0
        ).astype(BF16)
        acc[...] += jnp.dot(pick, delta_in[k], preferred_element_type=F32)
        return c

    load_w.wait()
    base(0, tok, True)
    load_dn.wait()
    load_up.wait()
    shrink(0, 0)
    gather(1, tok, 1, 1).wait_recv()
    base(1, gat.at[1], False)
    delta_in[0] = expand(0)
    add_delta(0, 0)

    lax.fori_loop(1, W // 2, arrive, 0)
    for j in range(2, T, 2):
        gather(j, tok, j, j).wait_recv()
        gather(j + 1, gat.at[j], j + 1, 1).start()
        base(j, gat.at[j], False)
    lax.fori_loop(1, W // 2, reply, 0)
    for j in range(2, T, 2):
        gather(j + 1, gat.at[j], j + 1, 1).wait_recv()
        base(j + 1, gat.at[j + 1], False)

    lax.fori_loop(W // 2, W, arrive, 0)
    lax.fori_loop(W // 2, W, reply, 0)

    def collect(k, c):
        delta_copy(k).wait_recv()
        return add_delta(k, c)

    lax.fori_loop(1, W, collect, 0)
    out[...] = acc[...].astype(BF16)

    def drain(k, c):
        loc_copy(k).wait_send()
        row_copy(k).wait_send()
        delta_copy(k).wait_send()
        return c

    lax.fori_loop(1, W, drain, 0)

    def drain_part(k, c):
        def one(j, c):
            part_copy(k, j).wait_send()
            return c

        return lax.fori_loop(1, T, one, c)

    lax.fori_loop(0, W, drain_part, 0)
    gather(1, tok, 1, 1).wait_send()
    for j in range(2, T, 2):
        gather(j, tok, j, j).wait_send()
        gather(j + 1, gat.at[j], j + 1, 1).wait_send()


def body(tokens, weight, down, up, adapter_per_row, table):
    R, F = tokens.shape
    W = lax.axis_size("wide")
    T = lax.axis_size("tensor")
    cap = 2 * R // W
    per_owner, rank = down.shape[1:]
    D, C = weight.shape
    N = per_owner * rank
    vmem = pl.BlockSpec(memory_space=pltpu.VMEM)
    hbm = pl.BlockSpec(memory_space=pl.ANY)
    dma = pltpu.SemaphoreType.DMA
    return pl.pallas_call(
        functools.partial(kernel, W, T, cap, per_owner, rank),
        out_shape=jax.ShapeDtypeStruct((R, C), BF16),
        in_specs=[vmem, hbm, hbm, hbm, vmem, vmem],
        out_specs=vmem,
        scratch_shapes=[
            pltpu.VMEM((D, C), BF16),
            pltpu.VMEM((F, N), BF16),
            pltpu.VMEM((N, C), BF16),
            pltpu.VMEM((T, R, F), BF16),
            pltpu.VMEM((R, C), F32),
            pltpu.VMEM((W, cap, F), BF16),
            pltpu.VMEM((W, cap, F), BF16),
            pltpu.VMEM((W, 8, LANES), F32),
            pltpu.VMEM((W, 8, LANES), F32),
            pltpu.VMEM((W, cap // 2, LANES), F32),
            pltpu.VMEM((W, T, cap // 2, LANES), F32),
            pltpu.VMEM((W, cap, C), BF16),
            pltpu.VMEM((W, cap, C), BF16),
            dma((3,)),
            dma((T,)),
            dma((T,)),
            dma((W,)),
            dma((W,)),
            dma((W,)),
            dma((W,)),
            dma((W, T)),
            dma((W, T)),
            dma((W,)),
            dma((W,)),
        ],
        compiler_params=pltpu.CompilerParams(
            collective_id=0, has_side_effects=True, vmem_limit_bytes=56 * 1024 * 1024
        ),
    )(
        tokens,
        weight,
        down.reshape(F, N),
        up.reshape(N, C),
        adapter_per_row.reshape(1, R),
        table.reshape(1, table.shape[0]),
    )


def solution(mesh):
    in_specs = (
        P("wide", "tensor"),
        P(None, "tensor"),
        P("tensor", "wide", None),
        P("wide", None, "tensor"),
        P("wide"),
        P(),
    )
    out_specs = P("wide", "tensor")
    return jax.shard_map(body, mesh=mesh, in_specs=in_specs, out_specs=out_specs, check_vma=False)
```

```python
import functools

import jax
import jax.numpy as jnp
from jax import lax
from jax.experimental import pallas as pl
from jax.experimental.pallas import tpu as pltpu
from jax.sharding import PartitionSpec as P

MESH = pl.DeviceIdType.MESH
F32 = jnp.float32
BF16 = jnp.bfloat16
LANES = 128


def flip(index, mask, count):
    out, bit = 0, 1
    while bit < count:
        out = out + ((index // bit + mask // bit) % 2) * bit
        bit *= 2
    return out


def iota(shape, dim):
    return lax.broadcasted_iota(jnp.int32, shape, dim)


def to_column(row, size):
    eye = iota((size, row.shape[1]), 0) == iota((size, row.shape[1]), 1)
    return jnp.sum(jnp.where(eye, row, 0.0), axis=1, keepdims=True)


def kernel(
    W,
    T,
    cap,
    per_owner,
    rank,
    tok,
    w_hbm,
    dn_hbm,
    up_hbm,
    apr,
    table,
    out,
    w,
    dn,
    up,
    gat,
    acc,
    rows_out,
    rows_in,
    loc_out,
    loc_in,
    part_out,
    part_in,
    delta_out,
    delta_in,
    load_sem,
    gat_s,
    gat_r,
    row_s,
    row_r,
    loc_s,
    loc_r,
    part_s,
    part_r,
    delta_s,
    delta_r,
):
    me = lax.axis_index("wide")
    te = lax.axis_index("tensor")
    R, F = tok.shape
    C = out.shape[1]
    A = table.shape[1]

    def wide_peer(k):
        return (flip(me, k, W), te)

    def tensor_peer(j):
        return (me, flip(te, j, T))

    barrier = pltpu.get_barrier_semaphore()

    def greet_wide(k, c):
        pl.semaphore_signal(barrier, inc=1, device_id=wide_peer(k), device_id_type=MESH)
        return c

    def greet_tensor(j, c):
        pl.semaphore_signal(barrier, inc=1, device_id=tensor_peer(j), device_id_type=MESH)
        return c

    lax.fori_loop(1, W, greet_wide, 0)
    lax.fori_loop(1, T, greet_tensor, 0)

    load_dn = pltpu.make_async_copy(dn_hbm, dn, load_sem.at[0])
    load_w = pltpu.make_async_copy(w_hbm, w, load_sem.at[1])
    load_up = pltpu.make_async_copy(up_hbm, up, load_sem.at[2])
    load_dn.start()
    load_w.start()
    load_up.start()

    entry = to_column(table[...].astype(F32), A)
    position = jnp.sum(jnp.where(iota((A, R), 0) == apr[...], entry, 0.0), axis=0, keepdims=True)
    owners = max(W, 16)
    owner_id = iota((owners, R), 0).astype(F32)
    hot = jnp.where(
        (position >= owner_id * per_owner) & (position < (owner_id + 1.0) * per_owner), 1.0, 0.0
    )
    before = jnp.where(iota((R, R), 0) < iota((R, R), 1), 1.0, 0.0).astype(BF16)
    earlier = jnp.dot(hot.astype(BF16), before, preferred_element_type=F32)
    owner = jnp.sum(hot * owner_id, axis=0, keepdims=True)
    slot = jnp.sum(hot * earlier, axis=0, keepdims=True) + owner * cap
    local = jnp.broadcast_to(position - owner * per_owner, (16, R)).astype(BF16)
    slot_column = to_column(slot, R)

    pl.semaphore_wait(barrier, W + T - 2)

    def gather(j, src, dst, peer):
        return pltpu.make_async_remote_copy(
            src_ref=src,
            dst_ref=gat.at[dst],
            send_sem=gat_s.at[j],
            recv_sem=gat_r.at[dst],
            device_id=tensor_peer(peer),
            device_id_type=MESH,
        )

    for j in range(2, T, 2):
        gather(j, tok, j, j).start()
    gather(1, tok, 1, 1).start()

    def row_copy(k):
        return pltpu.make_async_remote_copy(
            src_ref=rows_out.at[k],
            dst_ref=rows_in.at[k],
            send_sem=row_s.at[k],
            recv_sem=row_r.at[k],
            device_id=wide_peer(k),
            device_id_type=MESH,
        )

    def loc_copy(k):
        return pltpu.make_async_remote_copy(
            src_ref=loc_out.at[k],
            dst_ref=loc_in.at[k],
            send_sem=loc_s.at[k],
            recv_sem=loc_r.at[k],
            device_id=wide_peer(k),
            device_id_type=MESH,
        )

    def part_copy(k, j):
        return pltpu.make_async_remote_copy(
            src_ref=part_out.at[k],
            dst_ref=part_in.at[k, j],
            send_sem=part_s.at[k, j],
            recv_sem=part_r.at[k, j],
            device_id=tensor_peer(j),
            device_id_type=MESH,
        )

    def delta_copy(k):
        return pltpu.make_async_remote_copy(
            src_ref=delta_out.at[k],
            dst_ref=delta_in.at[k],
            send_sem=delta_s.at[k],
            recv_sem=delta_r.at[k],
            device_id=wide_peer(k),
            device_id_type=MESH,
        )

    def build(k, rows, loc):
        d = flip(me, k, W)
        size = max(cap, LANES)
        pick = jnp.where(
            (iota((size, R), 0) + d * cap).astype(F32) == slot, 1.0, 0.0
        ).astype(BF16)
        loc[k] = lax.dot_general(
            local, pick, (((1,), (1,)), ((), ())), preferred_element_type=F32
        )[:8, :LANES]
        step = min(512, F)
        for c in range(0, F, step):
            rows[k, :, c : c + step] = jnp.dot(
                pick[:cap], tok[:, c : c + step], preferred_element_type=F32
            ).astype(BF16)

    def send(k, c):
        build(k, rows_out, loc_out)
        loc_copy(k).start()
        row_copy(k).start()
        return c

    lax.fori_loop(W // 2, W, send, 0)
    lax.fori_loop(1, W // 2, send, 0)
    build(0, rows_in, loc_in)

    tile = min(256, C)

    def base(j, src, first):
        start = pl.multiple_of(flip(te, j, T) * F, F)

        def columns(n, c):
            cols = pl.ds(pl.multiple_of(n * tile, tile), tile)
            value = jnp.dot(src[...], w[pl.ds(start, F), cols], preferred_element_type=F32)
            if first:
                acc[:, cols] = value
            else:
                acc[:, cols] += value
            return c

        lax.fori_loop(0, C // tile, columns, 0)

    half = cap // 2
    lane = iota((cap, LANES), 1)
    upper = (lane >= rank).astype(F32)
    pairs = per_owner * rank // LANES

    def place(k):
        column = to_column(loc_in[k][:1, :], cap)
        pair = jnp.floor(column * 0.5)
        own = jnp.broadcast_to(column - 2.0 * pair, (cap, LANES)) == upper
        return pair, own

    def shrink(k, c):
        pair, own = place(k)
        total = jnp.zeros((cap, LANES), F32)
        for a in range(0, pairs, 2):
            value = lax.dot_general(
                rows_in[k],
                dn[a * LANES : (a + 2) * LANES],
                (((1,), (1,)), ((), ())),
                preferred_element_type=F32,
            )
            total += jnp.where(pair == a, value[:, :LANES], 0.0)
            total += jnp.where(pair == a + 1, value[:, LANES:], 0.0)
        total = jnp.where(own, total, 0.0)
        total += pltpu.roll(total, rank, 1)
        part_out[k] = jnp.where(lane[:half] < rank, total[:half], total[half:])

        def start(j, c):
            part_copy(k, j).start()
            return c

        return lax.fori_loop(1, T, start, c)

    def expand(k):
        def add(j, total):
            part_copy(k, j).wait_recv()
            return total + part_in[k, j]

        total = lax.fori_loop(1, T, add, part_out[k])
        other = pltpu.roll(total, rank, 1)
        low = lane[:half] < rank
        both = jnp.concatenate(
            [jnp.where(low, total, other), jnp.where(low, other, total)], axis=0
        )
        pair, own = place(k)
        both = jnp.where(own, both, 0.0)
        wide = jnp.concatenate(
            [jnp.where(pair == a, both, 0.0).astype(BF16) for a in range(pairs)], axis=1
        )
        return jnp.dot(wide, up[...], preferred_element_type=F32).astype(BF16)

    def arrive(k, c):
        loc_copy(k).wait_recv()
        row_copy(k).wait_recv()
        return shrink(k, c)

    def reply(k, c):
        delta_out[k] = expand(k)
        delta_copy(k).start()
        return c

    def add_delta(k, c):
        d = flip(me, k, W)
        pick = jnp.where(
            (iota((R, cap), 1) + d * cap).astype(F32) == slot_column, 1.0, 0.0
        ).astype(BF16)
        acc[...] += jnp.dot(pick, delta_in[k], preferred_element_type=F32)
        return c

    load_w.wait()
    base(0, tok, True)
    load_dn.wait()
    load_up.wait()
    shrink(0, 0)
    gather(1, tok, 1, 1).wait_recv()
    base(1, gat.at[1], False)
    delta_in[0] = expand(0)
    add_delta(0, 0)

    lax.fori_loop(1, W // 2, arrive, 0)
    for j in range(2, T, 2):
        gather(j, tok, j, j).wait_recv()
        gather(j + 1, gat.at[j], j + 1, 1).start()
        base(j, gat.at[j], False)
    lax.fori_loop(1, W // 2, reply, 0)
    for j in range(2, T, 2):
        gather(j + 1, gat.at[j], j + 1, 1).wait_recv()
        base(j + 1, gat.at[j + 1], False)

    def arrive_and_reply(k, c):
        arrive(k, c)
        return reply(k - 1, c)

    arrive(W // 2, 0)
    lax.fori_loop(W // 2 + 1, W, arrive_and_reply, 0)
    reply(W - 1, 0)

    def collect(k, c):
        delta_copy(k).wait_recv()
        return add_delta(k, c)

    lax.fori_loop(1, W, collect, 0)
    out[...] = acc[...].astype(BF16)

    def drain(k, c):
        loc_copy(k).wait_send()
        row_copy(k).wait_send()
        delta_copy(k).wait_send()
        return c

    lax.fori_loop(1, W, drain, 0)

    def drain_part(k, c):
        def one(j, c):
            part_copy(k, j).wait_send()
            return c

        return lax.fori_loop(1, T, one, c)

    lax.fori_loop(0, W, drain_part, 0)
    gather(1, tok, 1, 1).wait_send()
    for j in range(2, T, 2):
        gather(j, tok, j, j).wait_send()
        gather(j + 1, gat.at[j], j + 1, 1).wait_send()


def body(tokens, weight, down, up, adapter_per_row, table):
    R, F = tokens.shape
    W = lax.axis_size("wide")
    T = lax.axis_size("tensor")
    cap = 2 * R // W
    per_owner, rank = down.shape[1:]
    D, C = weight.shape
    N = per_owner * rank
    vmem = pl.BlockSpec(memory_space=pltpu.VMEM)
    hbm = pl.BlockSpec(memory_space=pl.ANY)
    dma = pltpu.SemaphoreType.DMA
    return pl.pallas_call(
        functools.partial(kernel, W, T, cap, per_owner, rank),
        out_shape=jax.ShapeDtypeStruct((R, C), BF16),
        in_specs=[vmem, hbm, hbm, hbm, vmem, vmem],
        out_specs=vmem,
        scratch_shapes=[
            pltpu.VMEM((D, C), BF16),
            pltpu.VMEM((N, F), BF16),
            pltpu.VMEM((N, C), BF16),
            pltpu.VMEM((T, R, F), BF16),
            pltpu.VMEM((R, C), F32),
            pltpu.VMEM((W, cap, F), BF16),
            pltpu.VMEM((W, cap, F), BF16),
            pltpu.VMEM((W, 8, LANES), F32),
            pltpu.VMEM((W, 8, LANES), F32),
            pltpu.VMEM((W, cap // 2, LANES), F32),
            pltpu.VMEM((W, T, cap // 2, LANES), F32),
            pltpu.VMEM((W, cap, C), BF16),
            pltpu.VMEM((W, cap, C), BF16),
            dma((3,)),
            dma((T,)),
            dma((T,)),
            dma((W,)),
            dma((W,)),
            dma((W,)),
            dma((W,)),
            dma((W, T)),
            dma((W, T)),
            dma((W,)),
            dma((W,)),
        ],
        compiler_params=pltpu.CompilerParams(
            collective_id=0, has_side_effects=True, vmem_limit_bytes=56 * 1024 * 1024
        ),
    )(
        tokens,
        weight,
        down.transpose(1, 2, 0).reshape(N, F),
        up.reshape(N, C),
        adapter_per_row.reshape(1, R),
        table.reshape(1, table.shape[0]),
    )


def solution(mesh):
    in_specs = (
        P("wide", "tensor"),
        P(None, "tensor"),
        P("tensor", "wide", None),
        P("wide", None, "tensor"),
        P("wide"),
        P(),
    )
    out_specs = P("wide", "tensor")
    return jax.shard_map(body, mesh=mesh, in_specs=in_specs, out_specs=out_specs, check_vma=False)
```
